128 devices in a mesh: grp: 32 (over x, z, core), tp: 4 (over y).
Axes of the slice: x: 4, y: 4, z: 4, core: 2. Of those that a mesh axis runs over, the one named last changes fastest.
Arguments:
- text_rows: bfloat16 [32768, 8192], P('grp', 'tp')
- image_rows: bfloat16 [16384, 8192], P('grp', 'tp')
- tile_slot: int32 [64], replicated, may hold values from 0 to 127, as said below
- seg_lengths: int32 [128], replicated, may hold values from 1 to 2048, 32768 in all
- norm_gain: bfloat16 [8192], P('tp'), may hold values from 0.5 to 1.5
- w_query: bfloat16 [8192, 4096], P('grp', 'tp'), may hold values from -0.0625 to 0.0625
- w_key: bfloat16 [8192, 1024], P(None, 'tp'), may hold values from -0.0625 to 0.0625
- w_value: bfloat16 [8192, 1024], P(None, 'tp'), may hold values from -0.0625 to 0.0625
- bias_query: float32 [4096], P('tp'), may hold values from -3 to 3
- bias_key: float32 [1024], P('tp'), may hold values from -3 to 3
- bias_value: float32 [1024], P('tp'), may hold values from -3 to 3
Outputs:
- query_out: bfloat16 [32768, 4096], P('grp', 'tp')
- key_out: bfloat16 [32768, 1024], P('grp', 'tp')
- value_out: bfloat16 [32768, 1024], P('grp', 'tp')
The draws below stay inside these ranges and needn't reach their ends.
Inputs may be any that keep to these rules, and one draw needn't show every extreme that they name: `tile_slot`: the 64 entries are distinct slots; tile t is encoded by group t // 2; slot p holds sequence positions 256 p to 256 p + 255; half of the slots hold an image tile. No encoder group has more than 2 blocks of 16 rows bound for one sequence shard, and some group has exactly 2. `seg_lengths`: the segments cover the sequence in order and sum to 32768.
All inputs are finite; a program needn't handle non-finite values.
Results may differ from the reference program's by a relative error of at most 0.0046.
Values may be sent and summed in bfloat16 or wider, within the bound.
No kernel may reach another device: no remote copies, remote signals or barrier semaphores. Data moves between devices by JAX's collectives and lax.ppermute only.
A program may use at most 128 MiB of HBM per device.

```python
import math
import jax
import jax.numpy as jnp
import numpy as np
from jax import lax

D = 8192
KVH = 8
QH = 32
HD = 128
BLK = 16
TILE = 256
ROWS_DEV = 1024
SEQ = 32768
TILES_G = 2
TILES = 64
SLOTS = 128
SLOT_STRIDE = 2
SEGS = 128
SEG_MOST = 2048
N_GRP = 32


def scaled_rows(key, row_count, spread, row_range):
    first_key, second_key, third_key = jax.random.split(key, 3)
    base = jax.random.normal(first_key, (row_count, D), dtype=jnp.float32)
    rough = jax.random.uniform(second_key, (D,), minval=0.5, maxval=2.0)
    row_scale = jnp.exp(jax.random.uniform(third_key, (row_count, 1), minval=0.0, maxval=math.log(row_range)))
    column = jnp.arange(D, dtype=jnp.float32) / D
    column_scale = jnp.exp(column * math.log(spread)) * rough
    return base * row_scale * column_scale[None, :]


def draw_text_rows(key, part):
    key = jax.random.fold_in(key, 11)
    return scaled_rows(key, SEQ, 10.0, 10.0).astype(jnp.bfloat16)


def draw_image_rows(key, part):
    key = jax.random.fold_in(key, 23)
    return scaled_rows(key, TILES * TILE, 10.0, 10.0).astype(jnp.bfloat16)


def draw_tile_slot(key, part):
    key = jax.random.fold_in(key, 37)
    first_key, second_key = jax.random.split(key)
    forced = (SLOT_STRIDE * jax.random.permutation(first_key, SLOTS // SLOT_STRIDE)[:TILES_G]).astype(jnp.int32)
    ranking = jax.random.permutation(second_key, SLOTS).astype(jnp.int32)
    taken = jnp.any(jnp.arange(SLOTS, dtype=jnp.int32)[:, None] == forced[None, :], axis=1)
    score = ranking + SLOTS * taken.astype(jnp.int32)
    remaining = jnp.argsort(score)[:TILES - TILES_G].astype(jnp.int32)
    return jnp.concatenate([forced, remaining]).astype(jnp.int32)


def levels(rng, extent, cuts, smallest, top_value):
    factor_of = 1.0
    for dim, blocks in cuts:
        heights = jax.random.uniform(jax.random.fold_in(jax.random.fold_in(rng, 6), dim), (blocks,), jnp.float32, smallest / len(cuts), top_value / len(cuts))
        factor_of = factor_of * jnp.repeat(jnp.exp(heights), extent[dim] // blocks).reshape((-1,) + (1,) * (len(extent) - 1 - dim))
    return factor_of


def split_up(count, total, limit, skew):
    portions = [(1 << 20) // math.isqrt(grade ** skew) + 1 for grade in range(2, count + 1)]
    spare, given = total - limit - (count - 1), [1] * (count - 1)
    while spare > 0:
        movable = [i for i in range(count - 1) if given[i] < limit]
        pool, left = sum([portions[i] for i in movable]), spare
        for i in movable:
            more = min(limit - given[i], max(1, left * portions[i] // pool), spare)
            given[i] = given[i] + more
            spare = spare - more
    return np.array([limit] + given)


def uneven(stream_key, number_of, total, bound, skew):
    if number_of == 2:
        one = jax.random.randint(stream_key, (), max(1, total - bound), min(bound, total - 1) + 1)
        return jnp.stack([one, total - one])
    tallies = jnp.asarray(split_up(number_of, total, bound, skew), jnp.int32)
    pairs = (number_of - 1) // 2
    giver, sink = tallies[1:1 + 2 * pairs:2], tallies[2:2 + 2 * pairs:2]
    slack = jnp.minimum(giver - 1, bound - sink)
    passed = jax.random.randint(jax.random.fold_in(stream_key, 1), (pairs,), 0, 1 << 20) % (slack + 1)
    tallies = tallies.at[1:1 + 2 * pairs:2].set(giver - passed).at[2:2 + 2 * pairs:2].set(sink + passed)
    return tallies[jax.random.permutation(jax.random.fold_in(stream_key, 2), number_of)]


def bell_draw(key, extent, scale, most, pieces=(), held_as=jnp.bfloat16):
    array = jax.random.normal(key, extent, jnp.float32) * scale
    if len(pieces) > 0:
        array = levels(key, extent, pieces, -0.22, 0.18) * array
    return jnp.clip(array, min=-most, max=most).astype(held_as)


def setup_inputs(seed: int = 0) -> dict:
    key_of = jax.random.split(jax.random.key(seed), 12)
    text_rows = draw_text_rows(jax.random.fold_in(key_of[11], 71), 0)
    image_rows = draw_image_rows(jax.random.fold_in(key_of[11], 71), 0)
    tile_slot = draw_tile_slot(jax.random.fold_in(key_of[11], 71), 0)
    seg_lengths = uneven(key_of[3], SEGS, SEQ, SEG_MOST, 2).astype(jnp.int32)
    norm_gain = jnp.clip(1.0 + 0.1 * jax.random.normal(key_of[4], (D,), jnp.float32), 0.5, 1.5).astype(jnp.bfloat16)
    w_query = bell_draw(key_of[5], (D, QH * HD), D ** -0.5, 0.0625, ((0, 32), (1, 4)))
    w_key = bell_draw(key_of[6], (D, KVH * HD), D ** -0.5, 0.0625, ((1, 4),))
    w_value = bell_draw(key_of[7], (D, KVH * HD), D ** -0.5, 0.0625, ((1, 4),))
    bias_query = bell_draw(key_of[8], (QH * HD,), 0.5, 3.0, ((0, 4),), jnp.float32)
    bias_key = bell_draw(key_of[9], (KVH * HD,), 0.5, 3.0, ((0, 4),), jnp.float32)
    bias_value = bell_draw(key_of[10], (KVH * HD,), 0.5, 3.0, ((0, 4),), jnp.float32)
    return {"text_rows": text_rows, "image_rows": image_rows, "tile_slot": tile_slot, "seg_lengths": seg_lengths, "norm_gain": norm_gain, "w_query": w_query, "w_key": w_key, "w_value": w_value, "bias_query": bias_query, "bias_key": bias_key, "bias_value": bias_value}


ROPE_THETA = 1000000.0
EPSILON = 1e-06

def rotate(values, positions):
    row_count = values.shape[0]
    head_count = values.shape[1] // HD
    half_width = HD // 2
    frequency = jnp.power(jnp.float32(ROPE_THETA), -jnp.arange(half_width, dtype=jnp.float32) * (2.0 / HD))
    angles = positions.astype(jnp.float32)[:, None] * frequency[None, :]
    cosine = jnp.cos(angles)[:, None, :]
    sine_part = jnp.sin(angles)[:, None, :]
    per_head = values.reshape(row_count, head_count, HD)
    lower_half = per_head[:, :, :half_width]
    upper_half = per_head[:, :, half_width:]
    rotated = jnp.concatenate([lower_half * cosine - upper_half * sine_part, upper_half * cosine + lower_half * sine_part], axis=2)
    return rotated.reshape(row_count, head_count * HD)

def reference(text_rows, image_rows, tile_slot, seg_lengths, norm_gain, w_query, w_key, w_value, bias_query, bias_key, bias_value):
    stored = jnp.arange(SEQ, dtype=jnp.int32)
    shard_index = stored // ROWS_DEV
    local_row = stored % ROWS_DEV
    sequence_pos = (local_row // BLK * N_GRP + shard_index) * BLK + local_row % BLK
    slot_match = (sequence_pos // TILE)[:, None] == tile_slot[None, :]
    present = jnp.any(slot_match, axis=1)
    tile_index = lax.optimization_barrier(jnp.sum(jnp.where(slot_match, jnp.arange(TILES, dtype=jnp.int32)[None, :], 0), axis=1)).astype(jnp.int32)
    source = tile_index * TILE + sequence_pos % TILE
    merged = jnp.where(present[:, None], image_rows[source], text_rows)
    seg_ends = jnp.cumsum(seg_lengths).astype(jnp.int32)
    seg_start = lax.optimization_barrier(jnp.sum(jnp.where(seg_ends[None, :] <= sequence_pos[:, None], seg_lengths[None, :], 0), axis=1)).astype(jnp.int32)
    position = (sequence_pos - seg_start).astype(jnp.int32)
    gain_full = norm_gain.astype(jnp.float32)

    def layer(block):
        rows_here, pos_here = block
        values = rows_here.astype(jnp.float32)
        inverse_rms = lax.rsqrt(lax.optimization_barrier(jnp.mean(values * values, axis=1, keepdims=True)) + EPSILON)
        normed = (values * inverse_rms * gain_full).astype(jnp.bfloat16)
        query_lin = jnp.dot(normed, w_query, preferred_element_type=jnp.float32) + bias_query
        key_lin = jnp.dot(normed, w_key, preferred_element_type=jnp.float32) + bias_key
        value_lin = jnp.dot(normed, w_value, preferred_element_type=jnp.float32) + bias_value
        return (rotate(query_lin, pos_here).astype(jnp.bfloat16), rotate(key_lin, pos_here).astype(jnp.bfloat16), value_lin.astype(jnp.bfloat16))
    results = lax.map(layer, (merged.reshape(N_GRP, ROWS_DEV, D), position.reshape(N_GRP, ROWS_DEV)))
    query_out = results[0].reshape(SEQ, QH * HD)
    key_out = results[1].reshape(SEQ, KVH * HD)
    value_out = results[2].reshape(SEQ, KVH * HD)
    return (query_out, key_out, value_out)
```

```python
import jax
import jax.numpy as jnp
from jax import lax
from jax.experimental import pallas as pl
from jax.experimental.pallas import tpu as pltpu
from jax.sharding import PartitionSpec as P

HD = 128
BLK = 16
TILE = 256
ROPE_THETA = 1000000.0
EPSILON = 1e-06

UP = [(i, (i + 1) % 4) for i in range(4)]
DOWN = [(i, (i + 3) % 4) for i in range(4)]
PAIRS = [(0, 1), (1, 0), (2, 3), (3, 2)]
MIRROR = [(0, 3), (3, 0), (1, 2), (2, 1)]
CUTS = (0, 24, 48, 64)
VMEM_LIMIT = 57 * 1024 * 1024
SPARE = 16


ACROSS = [(g, g ^ 16) for g in range(32)]


def params(**kw):
    return pltpu.CompilerParams(vmem_limit_bytes=VMEM_LIMIT, **kw)


ANY = pl.BlockSpec(memory_space=pl.ANY)


def pick_blocks(which, blocks):
    count = which.shape[0]

    def body(which_ref, src, dst, sem):
        def copy(i):
            return pltpu.make_async_copy(src.at[which_ref[i]], dst.at[i], sem.at[i])

        for i in range(count):
            copy(i).start()
        for i in range(count):
            copy(i).wait()

    return pl.pallas_call(
        body,
        out_shape=jax.ShapeDtypeStruct((count,) + blocks.shape[1:], blocks.dtype),
        grid_spec=pltpu.PrefetchScalarGridSpec(
            num_scalar_prefetch=1,
            grid=(1,),
            in_specs=[ANY],
            out_specs=pl.BlockSpec((count,) + blocks.shape[1:], lambda i, *_: (0, 0, 0)),
            scratch_shapes=[pltpu.SemaphoreType.DMA((count,))],
        ),
        compiler_params=params(),
        name="pick_blocks",
    )(which, blocks)


def rows_kernel(lo, hi, issue, scalars, smem, gain, sources, name):
    count = hi - lo
    half = count // 2
    feat = gain.shape[1]
    n_sc, n_src, n_sm = len(scalars), len(sources), len(smem)

    def body(*refs):
        scalar_refs, gain_ref, srcs = refs[:n_sc], refs[n_sc], refs[n_sc + 1 : n_sc + 1 + n_src]
        outs, (ss_ref, buf, sem) = refs[n_sc + 1 + n_src : n_sc + 3 + n_src], refs[n_sc + 3 + n_src : n_sc + 6 + n_src]

        def copy(src, block, i):
            pltpu.make_async_copy(src.at[block], buf.at[i], sem.at[i]).start()

        issue(scalar_refs, refs[n_sc + 6 + n_src :], srcs, copy)
        for part, out_ref in enumerate(outs):

            def work(i, carry):
                pltpu.make_async_copy(srcs[0].at[0], buf.at[part * half + i], sem.at[part * half + i]).wait()
                v = buf[part * half + i].astype(jnp.float32)
                ss_ref[pl.ds(pl.multiple_of((part * half + i) * BLK, BLK), BLK), :] = jnp.sum(v * v, axis=1, keepdims=True)
                out_ref[pl.ds(pl.multiple_of(i * BLK, BLK), BLK), :] = (v * gain_ref[...]).astype(jnp.bfloat16)
                return carry

            lax.fori_loop(0, half, work, 0)

    whole = lambda *shape: pl.BlockSpec(shape, lambda i, *_: (0,) * len(shape))
    return pl.pallas_call(
        body,
        out_shape=[jax.ShapeDtypeStruct((half * BLK, feat), jnp.bfloat16)] * 2
        + [jax.ShapeDtypeStruct((count * BLK, 1), jnp.float32)],
        grid_spec=pltpu.PrefetchScalarGridSpec(
            num_scalar_prefetch=n_sc,
            grid=(1,),
            in_specs=[whole(1, feat)] + [ANY] * n_src,
            out_specs=[whole(half * BLK, feat)] * 2 + [whole(count * BLK, 1)],
            scratch_shapes=[
                pltpu.VMEM((count, BLK, feat), jnp.bfloat16),
                pltpu.SemaphoreType.DMA((count,)),
            ]
            + smem,
        ),
        compiler_params=params(),
        name=name,
    )(*scalars, gain, *sources)


def first_rows(hi, tile_slot, half, gain, text):
    n_blocks = text.shape[0]

    def issue(scalar_refs, smem_refs, srcs, copy):
        slot_ref, half_ref = scalar_refs
        (taken,) = smem_refs

        def clear(j, carry):
            taken[j] = 0
            return carry

        def mark(t, carry):
            slot = slot_ref[t]

            @pl.when(lax.rem(slot, 2) == half_ref[0])
            def _():
                taken[lax.div(slot, 2)] = 1

            return carry

        def send(j, count):
            is_text = (taken[j] == 0) & (count < hi)

            @pl.when(is_text)
            def _():
                copy(srcs[0], j, count)

            return count + is_text.astype(jnp.int32)

        def fill(i, carry):
            copy(srcs[0], 0, i)
            return carry

        lax.fori_loop(0, n_blocks, clear, 0)
        lax.fori_loop(0, tile_slot.shape[0], mark, 0)
        lax.fori_loop(lax.fori_loop(0, n_blocks, send, 0), hi, fill, 0)

    smem = [pltpu.SMEM((n_blocks,), jnp.int32)]
    return rows_kernel(0, hi, issue, (tile_slot, half), smem, gain, [text], "first_rows")


def build(lo, hi, kinds, idxs, gain, text, arrived):
    n_src = 1 + len(arrived)

    def issue(scalar_refs, smem_refs, srcs, copy):
        kind_ref, idx_ref = scalar_refs

        def start(i, carry):
            kind = kind_ref[lo + i]
            for n in range(n_src):

                @pl.when((kind == n) | ((kind >= n_src) & (n == 0)))
                def _():
                    copy(srcs[n], idx_ref[lo + i], i)

            return carry

        lax.fori_loop(0, hi - lo, start, 0)

    return rows_kernel(lo, hi, issue, (kinds, idxs), [], gain, [text, *arrived], "build")


def near_sums(y, chunks, weights, wide):
    feat = chunks[0][0].shape[1]
    counts = [c[0].shape[0] for c in chunks]
    rows = sum(counts)
    tiles = [w.shape[1] // wide for w in weights]
    first = [sum(tiles[:i]) for i in range(len(tiles))]
    width = sum(tiles) * wide
    n_a, n_w = 3 * len(chunks), len(weights)

    def body(y_ref, *refs):
        acts, ws, out_ref = refs[:n_a], refs[n_a : n_a + 3 * n_w], refs[n_a + 3 * n_w]
        n = pl.program_id(0)
        for i in range(n_w):

            @pl.when((n >= first[i]) & (n < first[i] + tiles[i]))
            def _():
                for j, count in enumerate(counts):
                    at = sum(counts[:j])
                    total = None
                    for d in range(3):
                        term = jnp.dot(acts[3 * j + d][...], ws[3 * i + d][...], preferred_element_type=jnp.float32)
                        total = term if total is None else total + term
                    out_ref[at : at + count, :] = total

    def spec(i, d):
        return pl.BlockSpec(
            (feat, wide), lambda n, y_ref: (lax.rem(y_ref[0] + d, 4), jnp.clip(n - first[i], 0, tiles[i] - 1))
        )

    return pl.pallas_call(
        body,
        out_shape=jax.ShapeDtypeStruct((rows, width), jnp.float32),
        grid_spec=pltpu.PrefetchScalarGridSpec(
            num_scalar_prefetch=1,
            grid=(sum(tiles),),
            in_specs=[pl.BlockSpec((count, feat), lambda n, _: (0, 0)) for count in counts for _ in range(3)]
            + [spec(i, d) for i in range(n_w) for d in (0, 3, 1)],
            out_specs=pl.BlockSpec((rows, wide), lambda n, _: (0, n)),
        ),
        compiler_params=params(),
        cost_estimate=pl.CostEstimate(
            flops=6 * rows * feat * width, bytes_accessed=6 * feat * (width + rows), transcendentals=0
        ),
        name="near_sums",
    )(y, *[a for c in chunks for a in c], *[w for w in weights for _ in range(3)])


def finish(lo, hi, order, y, far, sums, weights, bias, inverse, cosine, sine, outs):
    wide = 256
    count = hi - lo
    rows = count * BLK
    row_count = cosine.shape[0]
    feat = far[0].shape[1]
    widths = [w.shape[1] for w in weights]
    tiles = [w // wide for w in widths]
    first = [sum(tiles[:i]) for i in range(3)]
    width = sum(widths)
    n_tiles = sum(tiles)
    n_f, n_s = len(far), len(sums)
    sum_tiles = [v.shape[1] // wide for v in sums]
    sum_first = [sum(sum_tiles[:i]) for i in range(n_s)]

    def body(order_ref, y_ref, *refs):
        fars, refs = refs[:n_f], refs[n_f:]
        sum_refs, refs = refs[:n_s], refs[n_s:]
        ws, (bias_ref, inv_ref, cos_ref, sin_ref) = refs[:3], refs[3:7]
        refs = refs[7 + len(outs) :]
        dst, stage, sem = refs[:3], refs[3:6], refs[6]
        n = pl.program_id(0)

        def move(i, which):
            to = pl.ds(pl.multiple_of(order_ref[lo + i] * BLK, BLK), BLK)
            return pltpu.make_async_copy(stage[which].at[i * BLK : i * BLK + BLK], dst[which].at[to], sem.at[which, i])

        for which in range(3):
            for tile in range(tiles[which]):
                step = first[which] + tile

                @pl.when(n == step)
                def _():
                    mine = max(i for i in range(n_s) if sum_first[i] <= step)
                    sum_ref = sum_refs[mine]
                    at = 0
                    for far_ref in fars:
                        here = slice(at, at + far_ref.shape[0])
                        there = slice(lo * BLK + here.start, lo * BLK + here.stop)
                        at = here.stop
                        total = sum_ref[here, :] + jnp.dot(
                            far_ref[...], ws[which][...], preferred_element_type=jnp.float32
                        )
                        inv = inv_ref[there, :]
                        for head in range(wide // HD):
                            cols = slice(head * HD, head * HD + HD)
                            val = jnp.where(inv > 0, total[:, cols] * inv, 0.0) + bias_ref[:, cols]
                            if which < 2:
                                val = val * cos_ref[there, :] + pltpu.roll(val, HD // 2, 1) * sin_ref[there, :]
                            col = tile * wide + head * HD
                            stage[which][here, col : col + HD] = val.astype(jnp.bfloat16)

                    if tile == tiles[which] - 1:
                        for i in range(count):
                            move(i, which).start()

        @pl.when(n == n_tiles - 1)
        def _():
            for which in range(3):
                for i in range(count):
                    move(i, which).wait()

    full = lambda *shape: pl.BlockSpec(shape, lambda n, *_: (0,) * len(shape))

    def far_rows(i):
        return pl.BlockSpec(
            (feat, wide),
            lambda n, order_ref, y_ref: (lax.rem(y_ref[0] + 2, 4), jnp.clip(n - first[i], 0, tiles[i] - 1)),
        )

    def sum_cols(i):
        return pl.BlockSpec((rows, wide), lambda n, *_: (0, jnp.clip(n - sum_first[i], 0, sum_tiles[i] - 1)))

    return pl.pallas_call(
        body,
        out_shape=[jax.ShapeDtypeStruct((row_count, w), jnp.bfloat16) for w in widths],
        grid_spec=pltpu.PrefetchScalarGridSpec(
            num_scalar_prefetch=2,
            grid=(n_tiles,),
            in_specs=[full(*f.shape) for f in far]
            + [sum_cols(i) for i in range(n_s)]
            + [far_rows(i) for i in range(3)]
            + [pl.BlockSpec((1, wide), lambda n, *_: (0, n))]
            + [full(row_count, HD)] * 3
            + [ANY] * len(outs),
            out_specs=[ANY] * 3,
            scratch_shapes=[pltpu.VMEM((rows, w), jnp.bfloat16) for w in widths]
            + [pltpu.SemaphoreType.DMA((3, count))],
        ),
        input_output_aliases={2 + n_f + n_s + 7 + i: i for i in range(len(outs))},
        compiler_params=params(),
        cost_estimate=pl.CostEstimate(
            flops=2 * rows * feat * width, bytes_accessed=2 * feat * (width + rows), transcendentals=0
        ),
        name="finish",
    )(order, y, *far, *sums, *weights, bias, inverse, cosine, sine, *outs)


def fast(
    text_rows, image_rows, tile_slot, seg_lengths, norm_gain, w_query, w_key, w_value, bias_query, bias_key, bias_value
):
    g = lax.axis_index("grp")
    y = lax.axis_index("tp")
    x = g // 8
    row_count, feat = text_rows.shape
    n_blocks = row_count // BLK
    scalar = lambda v: jnp.reshape(v, (1,)).astype(jnp.int32)

    parity = tile_slot % 2
    own_parity = lax.dynamic_slice_in_dim(parity, 2 * g, 1, 0)
    tile_rows = image_rows.reshape(2, 16 * BLK, feat)
    swapped = jnp.where(own_parity[:, None, None] == 0, tile_rows, tile_rows[::-1]).reshape(32, BLK, feat)
    block = jnp.arange(n_blocks, dtype=jnp.int32)
    tiles = jnp.arange(tile_slot.shape[0], dtype=jnp.int32)
    match = (2 * block + x // 2)[:, None] == tile_slot[None, :]
    pair = parity.reshape(32, 2)
    stray = pair[:, 0] == pair[:, 1]
    groups = jnp.arange(32, dtype=jnp.int32)
    alike = stray[None, :] & stray[:, None] & (pair[None, :, 0] == pair[:, None, 0]) & (groups[None, :] < groups[:, None])
    stray_rank = jnp.sum(alike.astype(jnp.int32), axis=1)
    to_forward = stray & (pair[:, 0] != x // 2)
    hit = to_forward[None, :] & (stray_rank[None, :] == jnp.arange(SPARE, dtype=jnp.int32)[:, None])
    forward = jnp.sum(jnp.where(hit, groups[None, :], 0), axis=1).astype(jnp.int32)
    stray_tile = jnp.stack([jnp.zeros_like(stray), stray], axis=1).reshape(-1)
    tile_kind = jnp.where(stray_tile, 2, 1)
    tile_index = jnp.where(stray_tile, jnp.repeat(stray_rank, 2), tiles // 2)
    kind = jnp.sum(jnp.where(match, tile_kind[None, :], 0), axis=1)
    from_tile = jnp.sum(jnp.where(match, tile_index[None, :], 0), axis=1)
    index = jnp.where(kind > 0, from_tile, block)
    key = kind * n_blocks + block
    rank = jnp.sum((key[None, :] < key[:, None]).astype(jnp.int32), axis=1)
    at = rank[None, :] == block[:, None]
    pick = lambda v: jnp.sum(jnp.where(at, v[None, :], 0), axis=1).astype(jnp.int32)
    order, kind, index = pick(block), pick(kind), pick(index)

    sequence_pos = ((order * 32 + g) * BLK)[:, None] + jnp.arange(BLK, dtype=jnp.int32)[None, :]
    sequence_pos = sequence_pos.reshape(-1)
    seg_ends = jnp.cumsum(seg_lengths)
    seg_start = jnp.sum(jnp.where(seg_ends[None, :] <= sequence_pos[:, None], seg_lengths[None, :], 0), axis=1)
    position = (sequence_pos - seg_start).astype(jnp.float32)
    frequency = jnp.power(jnp.float32(ROPE_THETA), -jnp.arange(HD // 2, dtype=jnp.float32) * (2.0 / HD))
    angles = position[:, None] * frequency[None, :]
    cosine, sine = jnp.cos(angles), jnp.sin(angles)
    cosine = jnp.concatenate([cosine, cosine], axis=1)
    sine = jnp.concatenate([-sine, sine], axis=1)

    gain = norm_gain.astype(jnp.float32)[None, :]
    text = text_rows.reshape(n_blocks, BLK, feat)
    bias = jnp.concatenate([bias_query, bias_key, bias_value])[None, :]
    me = scalar(y)
    squares = []

    def then(done, value):
        return lax.optimization_barrier((value, done))[0]

    def rows_of(n, arrived, after=None):
        if n == 0:
            top, bottom, ss = first_rows(CUTS[1], tile_slot, scalar(x // 2), gain, text)
        else:
            top, bottom, ss = build(CUTS[n], CUTS[n + 1], then(after, kind), index, gain, text, arrived)
        squares.append(ss[:, 0])
        return top, bottom

    def spread(halves):
        top, bottom = halves
        below_top = lax.ppermute(top, "tp", UP)
        above_bottom = lax.ppermute(bottom, "tp", DOWN)
        below_bottom = lax.ppermute(bottom, "tp", UP)
        above_top = lax.ppermute(top, "tp", DOWN)
        return (below_top, below_bottom), (above_top, above_bottom)

    def relay(below, above):
        return lax.ppermute(below[0], "tp", UP), lax.ppermute(above[1], "tp", DOWN)

    mine, near, far = [None] * 3, [None] * 3, [None] * 3
    mine[0] = rows_of(0, [])
    near[0] = spread(mine[0])
    came = lax.all_to_all(swapped, "grp", split_axis=0, concat_axis=0, tiled=True)
    wq = lax.all_gather(w_query, "grp", axis=0, tiled=True)
    far[0] = relay(*near[0])
    mine[1] = rows_of(1, [came], (near[0][0][0], near[0][1][1]))
    near[1] = spread(mine[1])
    picked = pick_blocks(then((mine[1], near[0]), forward), came)
    strays = lax.ppermute(picked, "grp", ACROSS)
    far[1] = relay(*near[1])
    weights_kv = (w_key, w_value)
    groups = [[(mine[0][i], near[0][0][i], near[0][1][i]) for i in range(2)]]
    kv_sums = [near_sums(then(picked, me), groups[0], weights_kv, 256)]
    mine[2] = rows_of(2, [came, strays], (far[0], near[1], kv_sums[0]))
    near[2] = spread(mine[2])
    far[2] = relay(*near[2])
    ss = jnp.concatenate(squares)
    ss = ss + lax.ppermute(ss, "tp", PAIRS)
    ss = ss + lax.ppermute(ss, "tp", MIRROR)
    inverse = jnp.broadcast_to(lax.rsqrt(ss / (4 * feat) + EPSILON)[:, None], (row_count, HD))
    groups += [[(mine[n][i], near[n][0][i], near[n][1][i]) for i in range(2)] for n in (1, 2)]
    kv_sums.append(near_sums(then(mine[2], me), groups[1], weights_kv, 256))
    early_kv = jnp.concatenate(kv_sums, axis=0)
    early_q = near_sums(then((kv_sums[1], far[1]), me), groups[0] + groups[1], (wq,), 256)
    weights = (wq, w_key, w_value)
    rest = (weights, bias, inverse, cosine, sine)
    outs = finish(CUTS[0], CUTS[2], order, me, far[0] + far[1], (early_q, early_kv), *rest, ())
    late = near_sums(then(outs[0], me), groups[2], weights, 256)
    outs = finish(CUTS[2], CUTS[3], order, me, far[2], (late,), *rest, tuple(outs))
    return tuple(outs)


def rotate(values, positions):
    row_count = values.shape[0]
    head_count = values.shape[1] // HD
    half_width = HD // 2
    frequency = jnp.power(jnp.float32(ROPE_THETA), -jnp.arange(half_width, dtype=jnp.float32) * (2.0 / HD))
    angles = positions.astype(jnp.float32)[:, None] * frequency[None, :]
    cosine = jnp.cos(angles)[:, None, :]
    sine_part = jnp.sin(angles)[:, None, :]
    per_head = values.reshape(row_count, head_count, HD)
    lower_half = per_head[:, :, :half_width]
    upper_half = per_head[:, :, half_width:]
    rotated = jnp.concatenate(
        [
            lower_half * cosine - upper_half * sine_part,
            upper_half * cosine + lower_half * sine_part,
        ],
        axis=2,
    )
    return rotated.reshape(row_count, head_count * HD)


def plain(
    text_rows, image_rows, tile_slot, seg_lengths, norm_gain, w_query, w_key, w_value, bias_query, bias_key, bias_value
):
    shard_index = lax.axis_index("grp")
    row_count, feat = text_rows.shape
    model_width = feat * 4
    blocks = image_rows.reshape(2, 16, BLK, feat).transpose(1, 0, 2, 3)
    arrived = lax.all_to_all(jnp.concatenate([blocks, blocks], axis=0), "grp", split_axis=0, concat_axis=0, tiled=True)
    arrived = arrived.reshape(64, BLK, feat)
    slot = 2 * jnp.arange(row_count // BLK, dtype=jnp.int32) + shard_index // 16
    slot_match = slot[:, None] == tile_slot[None, :]
    present = jnp.any(slot_match, axis=1)
    tile = jnp.sum(jnp.where(slot_match, jnp.arange(64, dtype=jnp.int32)[None, :], 0), axis=1)
    text_blocks = text_rows.reshape(row_count // BLK, BLK, feat)
    merged = jnp.where(present[:, None, None], arrived[tile], text_blocks).reshape(row_count, feat)
    row_index = jnp.arange(row_count, dtype=jnp.int32)
    sequence_pos = (row_index // BLK * 32 + shard_index) * BLK + row_index % BLK
    seg_ends = jnp.cumsum(seg_lengths)
    seg_start = jnp.sum(jnp.where(seg_ends[None, :] <= sequence_pos[:, None], seg_lengths[None, :], 0), axis=1)
    position = sequence_pos - seg_start
    values = merged.astype(jnp.float32)
    row_total = lax.psum(jnp.sum(values * values, axis=1), "tp")
    inverse_rms = lax.rsqrt(row_total[:, None] / model_width + EPSILON)
    normed_own = (values * inverse_rms * norm_gain.astype(jnp.float32)).astype(jnp.bfloat16)
    normed = lax.all_gather(normed_own, "tp", axis=1, tiled=True)
    dot = lambda w: jnp.dot(normed, w, preferred_element_type=jnp.float32)
    query_sum = dot(lax.all_gather(w_query, "grp", axis=0, tiled=True))
    query_out = rotate(query_sum + bias_query, position).astype(jnp.bfloat16)
    key_out = rotate(dot(w_key) + bias_key, position).astype(jnp.bfloat16)
    value_out = (dot(w_value) + bias_value).astype(jnp.bfloat16)
    return (query_out, key_out, value_out)


def shards(*args):
    tile_slot = args[2]
    pair = (tile_slot % 2).reshape(-1, 2)
    n_odd = jnp.sum(pair)
    both = jnp.sum((pair[:, 0] & pair[:, 1]))
    none = jnp.sum(((1 - pair[:, 0]) & (1 - pair[:, 1])))
    n_all = tile_slot.shape[0]
    fits = (jnp.minimum(n_odd, n_all - n_odd) >= CUTS[1]) & (jnp.maximum(both, none) <= min(SPARE, n_all - CUTS[2]))
    outs = fast(*args)
    return lax.cond(fits, lambda: outs, lambda: plain(*args))


def solution(mesh):
    in_specs = (
        P("grp", "tp"),
        P("grp", "tp"),
        P(),
        P(),
        P("tp"),
        P("grp", "tp"),
        P(None, "tp"),
        P(None, "tp"),
        P("tp"),
        P("tp"),
        P("tp"),
    )
    out_specs = (P("grp", "tp"), P("grp", "tp"), P("grp", "tp"))
    return jax.shard_map(shards, mesh=mesh, in_specs=in_specs, out_specs=out_specs, check_vma=False)
```

```python
import jax
import jax.numpy as jnp
from jax import lax
from jax.experimental import pallas as pl
from jax.experimental.pallas import tpu as pltpu
from jax.sharding import PartitionSpec as P

HD = 128
BLK = 16
TILE = 256
ROPE_THETA = 1000000.0
EPSILON = 1e-06

UP = [(i, (i + 1) % 4) for i in range(4)]
DOWN = [(i, (i + 3) % 4) for i in range(4)]
CUTS = (0, 24, 48, 64)
VMEM_LIMIT = 57 * 1024 * 1024
SPARE = 16


ACROSS = [(g, g ^ 16) for g in range(32)]


def params(**kw):
    return pltpu.CompilerParams(vmem_limit_bytes=VMEM_LIMIT, **kw)


ANY = pl.BlockSpec(memory_space=pl.ANY)


def pick_blocks(which, blocks):
    count = which.shape[0]

    def body(which_ref, src, dst, sem):
        def copy(i):
            return pltpu.make_async_copy(src.at[which_ref[i]], dst.at[i], sem.at[i])

        for i in range(count):
            copy(i).start()
        for i in range(count):
            copy(i).wait()

    return pl.pallas_call(
        body,
        out_shape=jax.ShapeDtypeStruct((count,) + blocks.shape[1:], blocks.dtype),
        grid_spec=pltpu.PrefetchScalarGridSpec(
            num_scalar_prefetch=1,
            grid=(1,),
            in_specs=[ANY],
            out_specs=pl.BlockSpec((count,) + blocks.shape[1:], lambda i, *_: (0, 0, 0)),
            scratch_shapes=[pltpu.SemaphoreType.DMA((count,))],
        ),
        compiler_params=params(),
        name="pick_blocks",
    )(which, blocks)


def rows_kernel(lo, hi, issue, scalars, smem, gain, sources, name, pieces=2):
    count = hi - lo
    half = count // pieces
    feat = gain.shape[1]
    n_sc, n_src, n_sm = len(scalars), len(sources), len(smem)

    def body(*refs):
        scalar_refs, gain_ref, srcs = refs[:n_sc], refs[n_sc], refs[n_sc + 1 : n_sc + 1 + n_src]
        refs_out = refs[n_sc + 1 + n_src :]
        outs, buf, sem = refs_out[:pieces], refs_out[pieces], refs_out[pieces + 1]

        def copy(src, block, i):
            pltpu.make_async_copy(src.at[block], buf.at[i], sem.at[i]).start()

        issue(scalar_refs, refs_out[pieces + 2 :], srcs, copy)
        for part, out_ref in enumerate(outs):

            def work(i, carry):
                pltpu.make_async_copy(srcs[0].at[0], buf.at[part * half + i], sem.at[part * half + i]).wait()
                v = buf[part * half + i].astype(jnp.float32)
                out_ref[pl.ds(pl.multiple_of(i * BLK, BLK), BLK), :] = (v * gain_ref[...]).astype(jnp.bfloat16)
                return carry

            lax.fori_loop(0, half, work, 0)

    whole = lambda *shape: pl.BlockSpec(shape, lambda i, *_: (0,) * len(shape))
    return pl.pallas_call(
        body,
        out_shape=[jax.ShapeDtypeStruct((half * BLK, feat), jnp.bfloat16)] * pieces,
        grid_spec=pltpu.PrefetchScalarGridSpec(
            num_scalar_prefetch=n_sc,
            grid=(1,),
            in_specs=[whole(1, feat)] + [ANY] * n_src,
            out_specs=[whole(half * BLK, feat)] * pieces,
            scratch_shapes=[
                pltpu.VMEM((count, BLK, feat), jnp.bfloat16),
                pltpu.SemaphoreType.DMA((count,)),
            ]
            + smem,
        ),
        compiler_params=params(),
        name=name,
    )(*scalars, gain, *sources)


def first_rows(hi, tile_slot, half, gain, text):
    n_blocks = text.shape[0]

    def issue(scalar_refs, smem_refs, srcs, copy):
        slot_ref, half_ref = scalar_refs
        (taken,) = smem_refs

        def clear(j, carry):
            taken[j] = 0
            return carry

        def mark(t, carry):
            slot = slot_ref[t]

            @pl.when(lax.rem(slot, 2) == half_ref[0])
            def _():
                taken[lax.div(slot, 2)] = 1

            return carry

        def send(j, count):
            is_text = (taken[j] == 0) & (count < hi)

            @pl.when(is_text)
            def _():
                copy(srcs[0], j, count)

            return count + is_text.astype(jnp.int32)

        def fill(i, carry):
            copy(srcs[0], 0, i)
            return carry

        lax.fori_loop(0, n_blocks, clear, 0)
        lax.fori_loop(0, tile_slot.shape[0], mark, 0)
        lax.fori_loop(lax.fori_loop(0, n_blocks, send, 0), hi, fill, 0)

    smem = [pltpu.SMEM((n_blocks,), jnp.int32)]
    return rows_kernel(0, hi, issue, (tile_slot, half), smem, gain, [text], "first_rows")


def build(lo, hi, kinds, idxs, gain, text, arrived, pieces=2):
    n_src = 1 + len(arrived)

    def issue(scalar_refs, smem_refs, srcs, copy):
        kind_ref, idx_ref = scalar_refs

        def start(i, carry):
            kind = kind_ref[lo + i]
            for n in range(n_src):

                @pl.when((kind == n) | ((kind >= n_src) & (n == 0)))
                def _():
                    copy(srcs[n], idx_ref[lo + i], i)

            return carry

        lax.fori_loop(0, hi - lo, start, 0)

    return rows_kernel(lo, hi, issue, (kinds, idxs), [], gain, [text, *arrived], "build", pieces)


def squares_of(act, unscale):
    v = act[...].astype(jnp.float32) * unscale
    return jnp.broadcast_to(jnp.sum(v * v, axis=1, keepdims=True), (act.shape[0], HD))


def near_sums(y, chunks, weights, wide, unscale=None):
    feat = chunks[0][0].shape[1]
    counts = [c[0].shape[0] for c in chunks]
    rows = sum(counts)
    tiles = [w.shape[1] // wide for w in weights]
    first = [sum(tiles[:i]) for i in range(len(tiles))]
    width = sum(tiles) * wide
    n_a, n_w = 3 * len(chunks), len(weights)
    n_u = 0 if unscale is None else 3

    def body(y_ref, *refs):
        acts, ws, refs = refs[:n_a], refs[n_a : n_a + 3 * n_w], refs[n_a + 3 * n_w :]
        out_ref = refs[n_u]
        n = pl.program_id(0)
        if n_u:

            @pl.when(n == 0)
            def _():
                for j, count in enumerate(counts):
                    at = sum(counts[:j])
                    parts = [squares_of(acts[3 * j + d], refs[d][0]) for d in range(3)]
                    refs[n_u + 1][at : at + count, :] = parts[0] + parts[1] + parts[2]

        for i in range(n_w):

            @pl.when((n >= first[i]) & (n < first[i] + tiles[i]))
            def _():
                for j, count in enumerate(counts):
                    at = sum(counts[:j])
                    total = None
                    for d in range(3):
                        term = jnp.dot(acts[3 * j + d][...], ws[3 * i + d][...], preferred_element_type=jnp.float32)
                        total = term if total is None else total + term
                    out_ref[at : at + count, :] = total

    def gain_spec(d):
        return pl.BlockSpec((1, 1, feat), lambda n, y_ref: (lax.rem(y_ref[0] + d, 4), 0, 0))

    def spec(i, d):
        return pl.BlockSpec(
            (feat, wide), lambda n, y_ref: (lax.rem(y_ref[0] + d, 4), jnp.clip(n - first[i], 0, tiles[i] - 1))
        )

    return pl.pallas_call(
        body,
        out_shape=[jax.ShapeDtypeStruct((rows, width), jnp.float32)]
        + [jax.ShapeDtypeStruct((rows, HD), jnp.float32)] * (n_u // 3),
        grid_spec=pltpu.PrefetchScalarGridSpec(
            num_scalar_prefetch=1,
            grid=(sum(tiles),),
            in_specs=[pl.BlockSpec((count, feat), lambda n, _: (0, 0)) for count in counts for _ in range(3)]
            + [spec(i, d) for i in range(n_w) for d in (0, 3, 1)]
            + [gain_spec(d) for d in (0, 3, 1)[:n_u]],
            out_specs=[pl.BlockSpec((rows, wide), lambda n, _: (0, n))]
            + [pl.BlockSpec((rows, HD), lambda n, _: (0, 0))] * (n_u // 3),
        ),
        compiler_params=params(),
        cost_estimate=pl.CostEstimate(
            flops=6 * rows * feat * width, bytes_accessed=6 * feat * (width + rows), transcendentals=0
        ),
        name="near_sums",
    )(y, *[a for c in chunks for a in c], *[w for w in weights for _ in range(3)], *[unscale] * n_u)


def finish(lo, hi, order, y, far, sums, weights, bias, squares, unscale, cosine, sine, outs):
    wide = 256
    count = hi - lo
    rows = count * BLK
    row_count = cosine.shape[0]
    feat = far[0].shape[1]
    widths = [w.shape[1] for w in weights]
    tiles = [w // wide for w in widths]
    first = [sum(tiles[:i]) for i in range(3)]
    width = sum(widths)
    n_tiles = sum(tiles)
    n_f, n_s = len(far), len(sums)
    sum_tiles = [v.shape[1] // wide for v in sums]
    sum_first = [sum(sum_tiles[:i]) for i in range(n_s)]

    def body(order_ref, y_ref, *refs):
        fars, refs = refs[:n_f], refs[n_f:]
        sum_refs, refs = refs[:n_s], refs[n_s:]
        ws, (bias_ref, ss_ref, unscale_ref, cos_ref, sin_ref) = refs[:3], refs[3:8]
        refs = refs[8 + len(outs) :]
        dst, stage, sem, inv_all = refs[:3], refs[3:6], refs[6], refs[7]
        n = pl.program_id(0)

        def move(i, which):
            to = pl.ds(pl.multiple_of(order_ref[lo + i] * BLK, BLK), BLK)
            return pltpu.make_async_copy(stage[which].at[i * BLK : i * BLK + BLK], dst[which].at[to], sem.at[which, i])

        @pl.when(n == 0)
        def _():
            at = 0
            for far_ref in fars:
                here = slice(at, at + far_ref.shape[0])
                at = here.stop
                total = ss_ref[here, :] + squares_of(far_ref, unscale_ref[0])
                inv_all[here, :] = lax.rsqrt(total * (1.0 / (4 * feat)) + EPSILON)

        for which in range(3):
            for tile in range(tiles[which]):
                step = first[which] + tile

                @pl.when(n == step)
                def _():
                    mine = max(i for i in range(n_s) if sum_first[i] <= step)
                    sum_ref = sum_refs[mine]
                    at = 0
                    for far_ref in fars:
                        here = slice(at, at + far_ref.shape[0])
                        there = slice(lo * BLK + here.start, lo * BLK + here.stop)
                        at = here.stop
                        total = sum_ref[here, :] + jnp.dot(
                            far_ref[...], ws[which][...], preferred_element_type=jnp.float32
                        )
                        inv = inv_all[here, :]
                        for head in range(wide // HD):
                            cols = slice(head * HD, head * HD + HD)
                            val = jnp.where(inv > 0, total[:, cols] * inv, 0.0) + bias_ref[:, cols]
                            if which < 2:
                                val = val * cos_ref[there, :] + pltpu.roll(val, HD // 2, 1) * sin_ref[there, :]
                            col = tile * wide + head * HD
                            stage[which][here, col : col + HD] = val.astype(jnp.bfloat16)

                    if tile == tiles[which] - 1:
                        for i in range(count):
                            move(i, which).start()

        @pl.when(n == n_tiles - 1)
        def _():
            for which in range(3):
                for i in range(count):
                    move(i, which).wait()

    full = lambda *shape: pl.BlockSpec(shape, lambda n, *_: (0,) * len(shape))

    def far_rows(i):
        return pl.BlockSpec(
            (feat, wide),
            lambda n, order_ref, y_ref: (lax.rem(y_ref[0] + 2, 4), jnp.clip(n - first[i], 0, tiles[i] - 1)),
        )

    def sum_cols(i):
        return pl.BlockSpec((rows, wide), lambda n, *_: (0, jnp.clip(n - sum_first[i], 0, sum_tiles[i] - 1)))

    return pl.pallas_call(
        body,
        out_shape=[jax.ShapeDtypeStruct((row_count, w), jnp.bfloat16) for w in widths],
        grid_spec=pltpu.PrefetchScalarGridSpec(
            num_scalar_prefetch=2,
            grid=(n_tiles,),
            in_specs=[full(*f.shape) for f in far]
            + [sum_cols(i) for i in range(n_s)]
            + [far_rows(i) for i in range(3)]
            + [pl.BlockSpec((1, wide), lambda n, *_: (0, n))]
            + [full(rows, HD), pl.BlockSpec((1, 1, feat), lambda n, o, y_ref: (lax.rem(y_ref[0] + 2, 4), 0, 0))]
            + [full(row_count, HD)] * 2
            + [ANY] * len(outs),
            out_specs=[ANY] * 3,
            scratch_shapes=[pltpu.VMEM((rows, w), jnp.bfloat16) for w in widths]
            + [pltpu.SemaphoreType.DMA((3, count)), pltpu.VMEM((rows, HD), jnp.float32)],
        ),
        input_output_aliases={2 + n_f + n_s + 8 + i: i for i in range(len(outs))},
        compiler_params=params(),
        cost_estimate=pl.CostEstimate(
            flops=2 * rows * feat * width, bytes_accessed=2 * feat * (width + rows), transcendentals=0
        ),
        name="finish",
    )(order, y, *far, *sums, *weights, bias, squares, unscale, cosine, sine, *outs)


def fast(
    text_rows, image_rows, tile_slot, seg_lengths, norm_gain, w_query, w_key, w_value, bias_query, bias_key, bias_value
):
    g = lax.axis_index("grp")
    y = lax.axis_index("tp")
    x = g // 8
    row_count, feat = text_rows.shape
    n_blocks = row_count // BLK
    scalar = lambda v: jnp.reshape(v, (1,)).astype(jnp.int32)

    parity = tile_slot % 2
    own_parity = lax.dynamic_slice_in_dim(parity, 2 * g, 1, 0)
    tile_rows = image_rows.reshape(2, 16 * BLK, feat)
    swapped = jnp.where(own_parity[:, None, None] == 0, tile_rows, tile_rows[::-1]).reshape(32, BLK, feat)
    block = jnp.arange(n_blocks, dtype=jnp.int32)
    tiles = jnp.arange(tile_slot.shape[0], dtype=jnp.int32)
    match = (2 * block + x // 2)[:, None] == tile_slot[None, :]
    pair = parity.reshape(32, 2)
    stray = pair[:, 0] == pair[:, 1]
    groups = jnp.arange(32, dtype=jnp.int32)
    alike = stray[None, :] & stray[:, None] & (pair[None, :, 0] == pair[:, None, 0]) & (groups[None, :] < groups[:, None])
    stray_rank = jnp.sum(alike.astype(jnp.int32), axis=1)
    to_forward = stray & (pair[:, 0] != x // 2)
    hit = to_forward[None, :] & (stray_rank[None, :] == jnp.arange(SPARE, dtype=jnp.int32)[:, None])
    forward = jnp.sum(jnp.where(hit, groups[None, :], 0), axis=1).astype(jnp.int32)
    stray_tile = jnp.stack([jnp.zeros_like(stray), stray], axis=1).reshape(-1)
    tile_kind = jnp.where(stray_tile, 2, 1)
    tile_index = jnp.where(stray_tile, jnp.minimum(jnp.repeat(stray_rank, 2), SPARE - 1), tiles // 2)
    kind = jnp.sum(jnp.where(match, tile_kind[None, :], 0), axis=1)
    from_tile = jnp.sum(jnp.where(match, tile_index[None, :], 0), axis=1)
    index = jnp.where(kind > 0, from_tile, block)
    key = kind * n_blocks + block
    rank = jnp.sum((key[None, :] < key[:, None]).astype(jnp.int32), axis=1)
    at = rank[None, :] == block[:, None]
    pick = lambda v: jnp.sum(jnp.where(at, v[None, :], 0), axis=1).astype(jnp.int32)
    order, kind, index = pick(block), pick(kind), pick(index)

    sequence_pos = ((order * 32 + g) * BLK)[:, None] + jnp.arange(BLK, dtype=jnp.int32)[None, :]
    sequence_pos = sequence_pos.reshape(-1)
    seg_ends = jnp.cumsum(seg_lengths)
    seg_start = jnp.sum(jnp.where(seg_ends[None, :] <= sequence_pos[:, None], seg_lengths[None, :], 0), axis=1)
    position = (sequence_pos - seg_start).astype(jnp.float32)
    frequency = jnp.power(jnp.float32(ROPE_THETA), -jnp.arange(HD // 2, dtype=jnp.float32) * (2.0 / HD))
    angles = position[:, None] * frequency[None, :]
    cosine, sine = jnp.cos(angles), jnp.sin(angles)
    cosine = jnp.concatenate([cosine, cosine], axis=1)
    sine = jnp.concatenate([-sine, sine], axis=1)

    gain = norm_gain.astype(jnp.float32)[None, :]
    text = text_rows.reshape(n_blocks, BLK, feat)
    bias = jnp.concatenate([bias_query, bias_key, bias_value])[None, :]
    me = scalar(y)

    def then(done, value):
        return lax.optimization_barrier((value, done))[0]

    def rows_of(n, arrived, after=None):
        if n == 0:
            return first_rows(CUTS[1], tile_slot, scalar(x // 2), gain, text)
        return build(CUTS[n], CUTS[n + 1], then(after, kind), index, gain, text, arrived, 2 if n == 1 else 1)

    def spread(halves):
        top, bottom = halves
        below_top = lax.ppermute(top, "tp", UP)
        above_bottom = lax.ppermute(bottom, "tp", DOWN)
        below_bottom = lax.ppermute(bottom, "tp", UP)
        above_top = lax.ppermute(top, "tp", DOWN)
        return (below_top, below_bottom), (above_top, above_bottom)

    def relay(below, above):
        return lax.ppermute(below[0], "tp", UP), lax.ppermute(above[1], "tp", DOWN)

    mine, near, far = [None] * 3, [None] * 3, [None] * 3
    mine[0] = rows_of(0, [])
    near[0] = spread(mine[0])
    came = lax.all_to_all(swapped, "grp", split_axis=0, concat_axis=0, tiled=True)
    wq = lax.all_gather(w_query, "grp", axis=0, tiled=True)
    late_gain = jnp.broadcast_to(then(came, norm_gain), (4, 1, feat))
    gains = lax.all_to_all(late_gain, "tp", split_axis=0, concat_axis=0, tiled=True)
    unscale = 1.0 / gains.astype(jnp.float32)
    far[0] = relay(*near[0])
    mine[1] = rows_of(1, [came], (near[0][0][0], near[0][1][1]))
    near[1] = spread(mine[1])
    picked = pick_blocks(then((mine[1], near[0]), forward), came)
    strays = lax.ppermute(picked, "grp", ACROSS)
    weights_kv = (w_key, w_value)
    groups = [[(mine[0][i], near[0][0][i], near[0][1][i]) for i in range(2)]]
    kv_sums, first_squares = near_sums(then((picked, far[0]), me), groups[0], weights_kv, 256, unscale)
    kv_sums, squares = [kv_sums], [first_squares]
    far[1] = relay(*then(first_squares, near[1]))
    groups.append([(mine[1][i], near[1][0][i], near[1][1][i]) for i in range(2)])
    sums, more_squares = near_sums(then(kv_sums[0], me), groups[1], weights_kv, 256, unscale)
    squares = jnp.concatenate([first_squares, more_squares], axis=0)
    early_kv = jnp.concatenate([kv_sums[0], sums], axis=0)
    mine[2] = rows_of(2, [came, strays], (far[0], far[1], early_kv, squares, bias, cosine, sine))
    near[2] = lax.ppermute(mine[2][0], "tp", UP), lax.ppermute(mine[2][0], "tp", DOWN)
    groups.append([(mine[2][0], *near[2])])
    (early_q,) = near_sums(then(mine[2], me), groups[0] + groups[1], (wq,), 256)
    middle = mine[2][0].shape[0] // 2
    below, above = then(early_q, near[2])
    far[2] = lax.ppermute(below[:middle], "tp", UP), lax.ppermute(above[middle:], "tp", DOWN)
    weights = (wq, w_key, w_value)
    rest = (unscale, cosine, sine)
    outs = finish(CUTS[0], CUTS[2], order, me, far[0] + far[1], (early_q, early_kv), weights, bias, squares, *rest, ())
    late, squares = near_sums(then(outs[0], me), groups[2], weights, 256, unscale)
    outs = finish(CUTS[2], CUTS[3], order, me, far[2], (late,), weights, bias, squares, *rest, tuple(outs))
    return tuple(outs)


def rotate(values, positions):
    row_count = values.shape[0]
    head_count = values.shape[1] // HD
    half_width = HD // 2
    frequency = jnp.power(jnp.float32(ROPE_THETA), -jnp.arange(half_width, dtype=jnp.float32) * (2.0 / HD))
    angles = positions.astype(jnp.float32)[:, None] * frequency[None, :]
    cosine = jnp.cos(angles)[:, None, :]
    sine_part = jnp.sin(angles)[:, None, :]
    per_head = values.reshape(row_count, head_count, HD)
    lower_half = per_head[:, :, :half_width]
    upper_half = per_head[:, :, half_width:]
    rotated = jnp.concatenate(
        [
            lower_half * cosine - upper_half * sine_part,
            upper_half * cosine + lower_half * sine_part,
        ],
        axis=2,
    )
    return rotated.reshape(row_count, head_count * HD)


def plain(
    text_rows, image_rows, tile_slot, seg_lengths, norm_gain, w_query, w_key, w_value, bias_query, bias_key, bias_value
):
    shard_index = lax.axis_index("grp")
    row_count, feat = text_rows.shape
    model_width = feat * 4
    blocks = image_rows.reshape(2, 16, BLK, feat).transpose(1, 0, 2, 3)
    arrived = lax.all_to_all(jnp.concatenate([blocks, blocks], axis=0), "grp", split_axis=0, concat_axis=0, tiled=True)
    arrived = arrived.reshape(64, BLK, feat)
    slot = 2 * jnp.arange(row_count // BLK, dtype=jnp.int32) + shard_index // 16
    slot_match = slot[:, None] == tile_slot[None, :]
    present = jnp.any(slot_match, axis=1)
    tile = jnp.sum(jnp.where(slot_match, jnp.arange(64, dtype=jnp.int32)[None, :], 0), axis=1)
    text_blocks = text_rows.reshape(row_count // BLK, BLK, feat)
    merged = jnp.where(present[:, None, None], arrived[tile], text_blocks).reshape(row_count, feat)
    row_index = jnp.arange(row_count, dtype=jnp.int32)
    sequence_pos = (row_index // BLK * 32 + shard_index) * BLK + row_index % BLK
    seg_ends = jnp.cumsum(seg_lengths)
    seg_start = jnp.sum(jnp.where(seg_ends[None, :] <= sequence_pos[:, None], seg_lengths[None, :], 0), axis=1)
    position = sequence_pos - seg_start
    values = merged.astype(jnp.float32)
    row_total = lax.psum(jnp.sum(values * values, axis=1), "tp")
    inverse_rms = lax.rsqrt(row_total[:, None] / model_width + EPSILON)
    normed_own = (values * inverse_rms * norm_gain.astype(jnp.float32)).astype(jnp.bfloat16)
    normed = lax.all_gather(normed_own, "tp", axis=1, tiled=True)
    dot = lambda w: jnp.dot(normed, w, preferred_element_type=jnp.float32)
    query_sum = dot(lax.all_gather(w_query, "grp", axis=0, tiled=True))
    query_out = rotate(query_sum + bias_query, position).astype(jnp.bfloat16)
    key_out = rotate(dot(w_key) + bias_key, position).astype(jnp.bfloat16)
    value_out = (dot(w_value) + bias_value).astype(jnp.bfloat16)
    return (query_out, key_out, value_out)


def shards(*args):
    tile_slot = args[2]
    pair = (tile_slot % 2).reshape(-1, 2)
    n_odd = jnp.sum(pair)
    both = jnp.sum((pair[:, 0] & pair[:, 1]))
    none = jnp.sum(((1 - pair[:, 0]) & (1 - pair[:, 1])))
    n_all = tile_slot.shape[0]
    fits = (jnp.minimum(n_odd, n_all - n_odd) >= CUTS[1]) & (jnp.maximum(both, none) <= min(SPARE, n_all - CUTS[2]))
    outs = fast(*args)
    return lax.cond(fits, lambda: outs, lambda: plain(*args))


def solution(mesh):
    in_specs = (
        P("grp", "tp"),
        P("grp", "tp"),
        P(),
        P(),
        P("tp"),
        P("grp", "tp"),
        P(None, "tp"),
        P(None, "tp"),
        P("tp"),
        P("tp"),
        P("tp"),
    )
    out_specs = (P("grp", "tp"), P("grp", "tp"), P("grp", "tp"))
    return jax.shard_map(shards, mesh=mesh, in_specs=in_specs, out_specs=out_specs, check_vma=False)
```

```python
import jax
import jax.numpy as jnp
from jax import lax
from jax.experimental import pallas as pl
from jax.experimental.pallas import tpu as pltpu
from jax.sharding import PartitionSpec as P

HD = 128
BLK = 16
TILE = 256
ROPE_THETA = 1000000.0
EPSILON = 1e-06

UP = [(i, (i + 1) % 4) for i in range(4)]
DOWN = [(i, (i + 3) % 4) for i in range(4)]
CUTS = (0, 24, 48, 64)
VMEM_LIMIT = 57 * 1024 * 1024
SPARE = 16


ACROSS = [(g, g ^ 16) for g in range(32)]


def params(**kw):
    return pltpu.CompilerParams(vmem_limit_bytes=VMEM_LIMIT, **kw)


ANY = pl.BlockSpec(memory_space=pl.ANY)


def pick_blocks(which, blocks):
    count = which.shape[0]

    def body(which_ref, src, dst, sem):
        def copy(i):
            return pltpu.make_async_copy(src.at[which_ref[i]], dst.at[i], sem.at[i])

        for i in range(count):
            copy(i).start()
        for i in range(count):
            copy(i).wait()

    return pl.pallas_call(
        body,
        out_shape=jax.ShapeDtypeStruct((count,) + blocks.shape[1:], blocks.dtype),
        grid_spec=pltpu.PrefetchScalarGridSpec(
            num_scalar_prefetch=1,
            grid=(1,),
            in_specs=[ANY],
            out_specs=pl.BlockSpec((count,) + blocks.shape[1:], lambda i, *_: (0, 0, 0)),
            scratch_shapes=[pltpu.SemaphoreType.DMA((count,))],
        ),
        compiler_params=params(),
        name="pick_blocks",
    )(which, blocks)


def rows_kernel(lo, hi, issue, scalars, smem, gain, sources, name, pieces=2):
    count = hi - lo
    half = count // pieces
    feat = gain.shape[1]
    n_sc, n_src, n_sm = len(scalars), len(sources), len(smem)

    def body(*refs):
        scalar_refs, gain_ref, srcs = refs[:n_sc], refs[n_sc], refs[n_sc + 1 : n_sc + 1 + n_src]
        refs_out = refs[n_sc + 1 + n_src :]
        outs, buf, sem = refs_out[:pieces], refs_out[pieces], refs_out[pieces + 1]

        def copy(src, block, i):
            pltpu.make_async_copy(src.at[block], buf.at[i], sem.at[i]).start()

        issue(scalar_refs, refs_out[pieces + 2 :], srcs, copy)
        for part, out_ref in enumerate(outs):

            def work(i, carry):
                pltpu.make_async_copy(srcs[0].at[0], buf.at[part * half + i], sem.at[part * half + i]).wait()
                v = buf[part * half + i].astype(jnp.float32)
                out_ref[pl.ds(pl.multiple_of(i * BLK, BLK), BLK), :] = (v * gain_ref[...]).astype(jnp.bfloat16)
                return carry

            lax.fori_loop(0, half, work, 0)

    whole = lambda *shape: pl.BlockSpec(shape, lambda i, *_: (0,) * len(shape))
    return pl.pallas_call(
        body,
        out_shape=[jax.ShapeDtypeStruct((half * BLK, feat), jnp.bfloat16)] * pieces,
        grid_spec=pltpu.PrefetchScalarGridSpec(
            num_scalar_prefetch=n_sc,
            grid=(1,),
            in_specs=[whole(1, feat)] + [ANY] * n_src,
            out_specs=[whole(half * BLK, feat)] * pieces,
            scratch_shapes=[
                pltpu.VMEM((count, BLK, feat), jnp.bfloat16),
                pltpu.SemaphoreType.DMA((count,)),
            ]
            + smem,
        ),
        compiler_params=params(),
        name=name,
    )(*scalars, gain, *sources)


def first_rows(hi, tile_slot, half, gain, text):
    n_blocks = text.shape[0]

    def issue(scalar_refs, smem_refs, srcs, copy):
        slot_ref, half_ref = scalar_refs
        (taken,) = smem_refs

        def clear(j, carry):
            taken[j] = 0
            return carry

        def mark(t, carry):
            slot = slot_ref[t]

            @pl.when(lax.rem(slot, 2) == half_ref[0])
            def _():
                taken[lax.div(slot, 2)] = 1

            return carry

        def send(j, count):
            is_text = (taken[j] == 0) & (count < hi)

            @pl.when(is_text)
            def _():
                copy(srcs[0], j, count)

            return count + is_text.astype(jnp.int32)

        def fill(i, carry):
            copy(srcs[0], 0, i)
            return carry

        lax.fori_loop(0, n_blocks, clear, 0)
        lax.fori_loop(0, tile_slot.shape[0], mark, 0)
        lax.fori_loop(lax.fori_loop(0, n_blocks, send, 0), hi, fill, 0)

    smem = [pltpu.SMEM((n_blocks,), jnp.int32)]
    return rows_kernel(0, hi, issue, (tile_slot, half), smem, gain, [text], "first_rows")


def build(lo, hi, kinds, idxs, gain, text, arrived, pieces=2):
    n_src = 1 + len(arrived)

    def issue(scalar_refs, smem_refs, srcs, copy):
        kind_ref, idx_ref = scalar_refs

        def start(i, carry):
            kind = kind_ref[lo + i]
            for n in range(n_src):

                @pl.when((kind == n) | ((kind >= n_src) & (n == 0)))
                def _():
                    copy(srcs[n], idx_ref[lo + i], i)

            return carry

        lax.fori_loop(0, hi - lo, start, 0)

    return rows_kernel(lo, hi, issue, (kinds, idxs), [], gain, [text, *arrived], "build", pieces)


def squares_of(act, unscale):
    v = act[...].astype(jnp.float32) * unscale
    return jnp.broadcast_to(jnp.sum(v * v, axis=1, keepdims=True), (act.shape[0], HD))


def near_sums(y, chunks, weights, wide, unscale=None):
    feat = chunks[0][0].shape[1]
    counts = [c[0].shape[0] for c in chunks]
    rows = sum(counts)
    tiles = [w.shape[1] // wide for w in weights]
    first = [sum(tiles[:i]) for i in range(len(tiles))]
    width = sum(tiles) * wide
    n_a, n_w = 3 * len(chunks), len(weights)
    n_u = 0 if unscale is None else 3

    def body(y_ref, *refs):
        acts, ws, refs = refs[:n_a], refs[n_a : n_a + 3 * n_w], refs[n_a + 3 * n_w :]
        out_ref = refs[n_u]
        n = pl.program_id(0)
        if n_u:

            @pl.when(n == 0)
            def _():
                for j, count in enumerate(counts):
                    at = sum(counts[:j])
                    parts = [squares_of(acts[3 * j + d], refs[d][0]) for d in range(3)]
                    refs[n_u + 1][at : at + count, :] = parts[0] + parts[1] + parts[2]

        for i in range(n_w):

            @pl.when((n >= first[i]) & (n < first[i] + tiles[i]))
            def _():
                for j, count in enumerate(counts):
                    at = sum(counts[:j])
                    total = None
                    for d in range(3):
                        term = jnp.dot(acts[3 * j + d][...], ws[3 * i + d][...], preferred_element_type=jnp.float32)
                        total = term if total is None else total + term
                    out_ref[at : at + count, :] = total

    def gain_spec(d):
        return pl.BlockSpec((1, 1, feat), lambda n, y_ref: (lax.rem(y_ref[0] + d, 4), 0, 0))

    def spec(i, d):
        return pl.BlockSpec(
            (feat, wide), lambda n, y_ref: (lax.rem(y_ref[0] + d, 4), jnp.clip(n - first[i], 0, tiles[i] - 1))
        )

    return pl.pallas_call(
        body,
        out_shape=[jax.ShapeDtypeStruct((rows, width), jnp.float32)]
        + [jax.ShapeDtypeStruct((rows, HD), jnp.float32)] * (n_u // 3),
        grid_spec=pltpu.PrefetchScalarGridSpec(
            num_scalar_prefetch=1,
            grid=(sum(tiles),),
            in_specs=[pl.BlockSpec((count, feat), lambda n, _: (0, 0)) for count in counts for _ in range(3)]
            + [spec(i, d) for i in range(n_w) for d in (0, 3, 1)]
            + [gain_spec(d) for d in (0, 3, 1)[:n_u]],
            out_specs=[pl.BlockSpec((rows, wide), lambda n, _: (0, n))]
            + [pl.BlockSpec((rows, HD), lambda n, _: (0, 0))] * (n_u // 3),
        ),
        compiler_params=params(),
        cost_estimate=pl.CostEstimate(
            flops=6 * rows * feat * width, bytes_accessed=6 * feat * (width + rows), transcendentals=0
        ),
        name="near_sums",
    )(y, *[a for c in chunks for a in c], *[w for w in weights for _ in range(3)], *[unscale] * n_u)


def finish(lo, hi, order, y, far, sums, weights, bias, squares, unscale, cosine, sine, outs, near=()):
    wide = 256
    count = hi - lo
    rows = count * BLK
    row_count = cosine.shape[0]
    feat = far[0].shape[1]
    widths = [w.shape[1] for w in weights]
    tiles = [w // wide for w in widths]
    first = [sum(tiles[:i]) for i in range(3)]
    width = sum(widths)
    n_tiles = sum(tiles)
    n_f, n_s, n_n = len(far), len(sums), len(near)
    places = (0, 3, 1)[:n_n]
    sum_tiles = [v.shape[1] // wide for v in sums]
    sum_first = [sum(sum_tiles[:i]) for i in range(n_s)]

    def body(order_ref, y_ref, *refs):
        fars, refs = refs[:n_f], refs[n_f:]
        sum_refs, refs = refs[:n_s], refs[n_s:]
        near_refs, refs = refs[:n_n], refs[n_n:]
        near_ws, refs = refs[: 3 * n_n], refs[3 * n_n :]
        near_unscale, refs = refs[:n_n], refs[n_n:]
        ss_refs, refs = refs[:n_s and 1], refs[n_s and 1 :]
        ws, (bias_ref, unscale_ref, cos_ref, sin_ref) = refs[:3], refs[3:7]
        refs = refs[7 + len(outs) :]
        dst, stage, sem, inv_all = refs[:3], refs[3:6], refs[6], refs[7]
        n = pl.program_id(0)

        def move(i, which):
            to = pl.ds(pl.multiple_of(order_ref[lo + i] * BLK, BLK), BLK)
            return pltpu.make_async_copy(stage[which].at[i * BLK : i * BLK + BLK], dst[which].at[to], sem.at[which, i])

        @pl.when(n == 0)
        def _():
            at = 0
            for far_ref in fars:
                here = slice(at, at + far_ref.shape[0])
                at = here.stop
                total = squares_of(far_ref, unscale_ref[0])
                for ref in ss_refs:
                    total += ref[here, :]
                for ref, by in zip(near_refs, near_unscale):
                    total += squares_of(ref.at[here], by[0])
                inv_all[here, :] = lax.rsqrt(total * (1.0 / (4 * feat)) + EPSILON)

        for which in range(3):
            for tile in range(tiles[which]):
                step = first[which] + tile

                @pl.when(n == step)
                def _():
                    if n_n:
                        begun = None
                        for d in range(n_n):
                            term = jnp.dot(near_refs[d][...], near_ws[3 * d + which][...], preferred_element_type=jnp.float32)
                            begun = term if begun is None else begun + term
                    else:
                        begun = sum_refs[max(i for i in range(n_s) if sum_first[i] <= step)]
                    at = 0
                    for far_ref in fars:
                        here = slice(at, at + far_ref.shape[0])
                        there = slice(lo * BLK + here.start, lo * BLK + here.stop)
                        at = here.stop
                        total = begun[here, :] + jnp.dot(
                            far_ref[...], ws[which][...], preferred_element_type=jnp.float32
                        )
                        inv = inv_all[here, :]
                        for head in range(wide // HD):
                            cols = slice(head * HD, head * HD + HD)
                            val = jnp.where(inv > 0, total[:, cols] * inv, 0.0) + bias_ref[:, cols]
                            if which < 2:
                                val = val * cos_ref[there, :] + pltpu.roll(val, HD // 2, 1) * sin_ref[there, :]
                            col = tile * wide + head * HD
                            stage[which][here, col : col + HD] = val.astype(jnp.bfloat16)

                    if tile == tiles[which] - 1:
                        for i in range(count):
                            move(i, which).start()

        @pl.when(n == n_tiles - 1)
        def _():
            for which in range(3):
                for i in range(count):
                    move(i, which).wait()

    full = lambda *shape: pl.BlockSpec(shape, lambda n, *_: (0,) * len(shape))

    def far_rows(i, d=2):
        return pl.BlockSpec(
            (feat, wide),
            lambda n, order_ref, y_ref: (lax.rem(y_ref[0] + d, 4), jnp.clip(n - first[i], 0, tiles[i] - 1)),
        )

    def gain_rows(d):
        return pl.BlockSpec((1, 1, feat), lambda n, o, y_ref: (lax.rem(y_ref[0] + d, 4), 0, 0))

    def sum_cols(i):
        return pl.BlockSpec((rows, wide), lambda n, *_: (0, jnp.clip(n - sum_first[i], 0, sum_tiles[i] - 1)))

    return pl.pallas_call(
        body,
        out_shape=[jax.ShapeDtypeStruct((row_count, w), jnp.bfloat16) for w in widths],
        grid_spec=pltpu.PrefetchScalarGridSpec(
            num_scalar_prefetch=2,
            grid=(n_tiles,),
            in_specs=[full(*f.shape) for f in far]
            + [sum_cols(i) for i in range(n_s)]
            + [full(rows, feat) for _ in near]
            + [far_rows(i, d) for d in places for i in range(3)]
            + [gain_rows(d) for d in places]
            + [full(rows, HD)] * (n_s and 1)
            + [far_rows(i) for i in range(3)]
            + [pl.BlockSpec((1, wide), lambda n, *_: (0, n))]
            + [gain_rows(2)]
            + [full(row_count, HD)] * 2
            + [ANY] * len(outs),
            out_specs=[ANY] * 3,
            scratch_shapes=[pltpu.VMEM((rows, w), jnp.bfloat16) for w in widths]
            + [pltpu.SemaphoreType.DMA((3, count)), pltpu.VMEM((rows, HD), jnp.float32)],
        ),
        input_output_aliases={2 + n_f + n_s + (n_s and 1) + 5 * n_n + 7 + i: i for i in range(len(outs))},
        compiler_params=params(),
        cost_estimate=pl.CostEstimate(
            flops=2 * rows * feat * width, bytes_accessed=2 * feat * (width + rows), transcendentals=0
        ),
        name="finish",
    )(
        order,
        y,
        *far,
        *sums,
        *near,
        *[w for _ in near for w in weights],
        *[unscale for _ in near],
        *[squares][: n_s and 1],
        *weights,
        bias,
        unscale,
        cosine,
        sine,
        *outs,
    )


def fast(
    text_rows, image_rows, tile_slot, seg_lengths, norm_gain, w_query, w_key, w_value, bias_query, bias_key, bias_value
):
    g = lax.axis_index("grp")
    y = lax.axis_index("tp")
    x = g // 8
    row_count, feat = text_rows.shape
    n_blocks = row_count // BLK
    scalar = lambda v: jnp.reshape(v, (1,)).astype(jnp.int32)

    parity = tile_slot % 2
    own_parity = lax.dynamic_slice_in_dim(parity, 2 * g, 1, 0)
    tile_rows = image_rows.reshape(2, 16 * BLK, feat)
    swapped = jnp.where(own_parity[:, None, None] == 0, tile_rows, tile_rows[::-1]).reshape(32, BLK, feat)
    block = jnp.arange(n_blocks, dtype=jnp.int32)
    tiles = jnp.arange(tile_slot.shape[0], dtype=jnp.int32)
    match = (2 * block + x // 2)[:, None] == tile_slot[None, :]
    pair = parity.reshape(32, 2)
    stray = pair[:, 0] == pair[:, 1]
    groups = jnp.arange(32, dtype=jnp.int32)
    alike = stray[None, :] & stray[:, None] & (pair[None, :, 0] == pair[:, None, 0]) & (groups[None, :] < groups[:, None])
    stray_rank = jnp.sum(alike.astype(jnp.int32), axis=1)
    to_forward = stray & (pair[:, 0] != x // 2)
    hit = to_forward[None, :] & (stray_rank[None, :] == jnp.arange(SPARE, dtype=jnp.int32)[:, None])
    forward = jnp.sum(jnp.where(hit, groups[None, :], 0), axis=1).astype(jnp.int32)
    stray_tile = jnp.stack([jnp.zeros_like(stray), stray], axis=1).reshape(-1)
    tile_kind = jnp.where(stray_tile, 2, 1)
    tile_index = jnp.where(stray_tile, jnp.minimum(jnp.repeat(stray_rank, 2), SPARE - 1), tiles // 2)
    kind = jnp.sum(jnp.where(match, tile_kind[None, :], 0), axis=1)
    from_tile = jnp.sum(jnp.where(match, tile_index[None, :], 0), axis=1)
    index = jnp.where(kind > 0, from_tile, block)
    key = kind * n_blocks + block
    rank = jnp.sum((key[None, :] < key[:, None]).astype(jnp.int32), axis=1)
    at = rank[None, :] == block[:, None]
    pick = lambda v: jnp.sum(jnp.where(at, v[None, :], 0), axis=1).astype(jnp.int32)
    order, kind, index = pick(block), pick(kind), pick(index)

    sequence_pos = ((order * 32 + g) * BLK)[:, None] + jnp.arange(BLK, dtype=jnp.int32)[None, :]
    sequence_pos = sequence_pos.reshape(-1)
    seg_ends = jnp.cumsum(seg_lengths)
    seg_start = jnp.sum(jnp.where(seg_ends[None, :] <= sequence_pos[:, None], seg_lengths[None, :], 0), axis=1)
    position = (sequence_pos - seg_start).astype(jnp.float32)
    frequency = jnp.power(jnp.float32(ROPE_THETA), -jnp.arange(HD // 2, dtype=jnp.float32) * (2.0 / HD))
    angles = position[:, None] * frequency[None, :]
    cosine, sine = jnp.cos(angles), jnp.sin(angles)
    cosine = jnp.concatenate([cosine, cosine], axis=1)
    sine = jnp.concatenate([-sine, sine], axis=1)

    gain = norm_gain.astype(jnp.float32)[None, :]
    text = text_rows.reshape(n_blocks, BLK, feat)
    bias = jnp.concatenate([bias_query, bias_key, bias_value])[None, :]
    me = scalar(y)

    def then(done, value):
        return lax.optimization_barrier((value, done))[0]

    def rows_of(n, arrived, after=None):
        if n == 0:
            return first_rows(CUTS[1], tile_slot, scalar(x // 2), gain, text)
        return build(CUTS[n], CUTS[n + 1], then(after, kind), index, gain, text, arrived, 2 if n == 1 else 1)

    def spread(halves):
        top, bottom = halves
        below_top = lax.ppermute(top, "tp", UP)
        above_bottom = lax.ppermute(bottom, "tp", DOWN)
        below_bottom = lax.ppermute(bottom, "tp", UP)
        above_top = lax.ppermute(top, "tp", DOWN)
        return (below_top, below_bottom), (above_top, above_bottom)

    def relay(below, above):
        return lax.ppermute(below[0], "tp", UP), lax.ppermute(above[1], "tp", DOWN)

    mine, near, far = [None] * 3, [None] * 3, [None] * 3
    mine[0] = rows_of(0, [])
    near[0] = spread(mine[0])
    came = lax.all_to_all(swapped, "grp", split_axis=0, concat_axis=0, tiled=True)
    wq = lax.all_gather(w_query, "grp", axis=0, tiled=True)
    late_gain = jnp.broadcast_to(then(came, norm_gain), (4, 1, feat))
    gains = lax.all_to_all(late_gain, "tp", split_axis=0, concat_axis=0, tiled=True)
    unscale = 1.0 / gains.astype(jnp.float32)
    far[0] = relay(*near[0])
    mine[1] = rows_of(1, [came], (near[0][0][0], near[0][1][1]))
    near[1] = spread(mine[1])
    picked = pick_blocks(then((mine[1], near[0]), forward), came)
    strays = lax.ppermute(picked, "grp", ACROSS)
    weights_kv = (w_key, w_value)
    groups = [[(mine[0][i], near[0][0][i], near[0][1][i]) for i in range(2)]]
    kv_sums, first_squares = near_sums(then((picked, far[0]), me), groups[0], weights_kv, 256, unscale)
    kv_sums, squares = [kv_sums], [first_squares]
    far[1] = relay(*then(first_squares, near[1]))
    groups.append([(mine[1][i], near[1][0][i], near[1][1][i]) for i in range(2)])
    sums, more_squares = near_sums(then(kv_sums[0], me), groups[1], weights_kv, 256, unscale)
    squares = jnp.concatenate([first_squares, more_squares], axis=0)
    early_kv = jnp.concatenate([kv_sums[0], sums], axis=0)
    mine[2] = rows_of(2, [came, strays], (far[0], far[1], early_kv, squares, bias, cosine, sine))
    near[2] = lax.ppermute(mine[2][0], "tp", UP), lax.ppermute(mine[2][0], "tp", DOWN)
    groups.append([(mine[2][0], *near[2])])
    (early_q,) = near_sums(then(mine[2], me), groups[0] + groups[1], (wq,), 256)
    middle = mine[2][0].shape[0] // 2
    below, above = then(early_q, near[2])
    far[2] = lax.ppermute(below[:middle], "tp", UP), lax.ppermute(above[middle:], "tp", DOWN)
    weights = (wq, w_key, w_value)
    rest = (unscale, cosine, sine)
    outs = finish(CUTS[0], CUTS[2], order, me, far[0] + far[1], (early_q, early_kv), weights, bias, squares, *rest, ())
    outs = finish(CUTS[2], CUTS[3], order, me, far[2], (), weights, bias, None, *rest, tuple(outs), groups[2][0])
    return tuple(outs)


def rotate(values, positions):
    row_count = values.shape[0]
    head_count = values.shape[1] // HD
    half_width = HD // 2
    frequency = jnp.power(jnp.float32(ROPE_THETA), -jnp.arange(half_width, dtype=jnp.float32) * (2.0 / HD))
    angles = positions.astype(jnp.float32)[:, None] * frequency[None, :]
    cosine = jnp.cos(angles)[:, None, :]
    sine_part = jnp.sin(angles)[:, None, :]
    per_head = values.reshape(row_count, head_count, HD)
    lower_half = per_head[:, :, :half_width]
    upper_half = per_head[:, :, half_width:]
    rotated = jnp.concatenate(
        [
            lower_half * cosine - upper_half * sine_part,
            upper_half * cosine + lower_half * sine_part,
        ],
        axis=2,
    )
    return rotated.reshape(row_count, head_count * HD)


def plain(
    text_rows, image_rows, tile_slot, seg_lengths, norm_gain, w_query, w_key, w_value, bias_query, bias_key, bias_value
):
    shard_index = lax.axis_index("grp")
    row_count, feat = text_rows.shape
    model_width = feat * 4
    blocks = image_rows.reshape(2, 16, BLK, feat).transpose(1, 0, 2, 3)
    arrived = lax.all_to_all(jnp.concatenate([blocks, blocks], axis=0), "grp", split_axis=0, concat_axis=0, tiled=True)
    arrived = arrived.reshape(64, BLK, feat)
    slot = 2 * jnp.arange(row_count // BLK, dtype=jnp.int32) + shard_index // 16
    slot_match = slot[:, None] == tile_slot[None, :]
    present = jnp.any(slot_match, axis=1)
    tile = jnp.sum(jnp.where(slot_match, jnp.arange(64, dtype=jnp.int32)[None, :], 0), axis=1)
    text_blocks = text_rows.reshape(row_count // BLK, BLK, feat)
    merged = jnp.where(present[:, None, None], arrived[tile], text_blocks).reshape(row_count, feat)
    row_index = jnp.arange(row_count, dtype=jnp.int32)
    sequence_pos = (row_index // BLK * 32 + shard_index) * BLK + row_index % BLK
    seg_ends = jnp.cumsum(seg_lengths)
    seg_start = jnp.sum(jnp.where(seg_ends[None, :] <= sequence_pos[:, None], seg_lengths[None, :], 0), axis=1)
    position = sequence_pos - seg_start
    values = merged.astype(jnp.float32)
    row_total = lax.psum(jnp.sum(values * values, axis=1), "tp")
    inverse_rms = lax.rsqrt(row_total[:, None] / model_width + EPSILON)
    normed_own = (values * inverse_rms * norm_gain.astype(jnp.float32)).astype(jnp.bfloat16)
    normed = lax.all_gather(normed_own, "tp", axis=1, tiled=True)
    dot = lambda w: jnp.dot(normed, w, preferred_element_type=jnp.float32)
    query_sum = dot(lax.all_gather(w_query, "grp", axis=0, tiled=True))
    query_out = rotate(query_sum + bias_query, position).astype(jnp.bfloat16)
    key_out = rotate(dot(w_key) + bias_key, position).astype(jnp.bfloat16)
    value_out = (dot(w_value) + bias_value).astype(jnp.bfloat16)
    return (query_out, key_out, value_out)


def shards(*args):
    tile_slot = args[2]
    pair = (tile_slot % 2).reshape(-1, 2)
    n_odd = jnp.sum(pair)
    both = jnp.sum((pair[:, 0] & pair[:, 1]))
    none = jnp.sum(((1 - pair[:, 0]) & (1 - pair[:, 1])))
    n_all = tile_slot.shape[0]
    fits = (jnp.minimum(n_odd, n_all - n_odd) >= CUTS[1]) & (jnp.maximum(both, none) <= min(SPARE, n_all - CUTS[2]))
    outs = fast(*args)
    return lax.cond(fits, lambda: outs, lambda: plain(*args))


def solution(mesh):
    in_specs = (
        P("grp", "tp"),
        P("grp", "tp"),
        P(),
        P(),
        P("tp"),
        P("grp", "tp"),
        P(None, "tp"),
        P(None, "tp"),
        P("tp"),
        P("tp"),
        P("tp"),
    )
    out_specs = (P("grp", "tp"), P("grp", "tp"), P("grp", "tp"))
    return jax.shard_map(shards, mesh=mesh, in_specs=in_specs, out_specs=out_specs, check_vma=False)
```
